512 devices in a mesh: sess: 16 (over y, core), band: 32 (over x, z).
Axes of the slice: x: 4, y: 8, z: 8, core: 2. Of those that a mesh axis runs over, the one named last changes fastest.
Arguments:
- frame: bfloat16 [64, 96, 128, 128], P('sess', None, 'band'), may hold values from -40 to 40
- cache: bfloat16 [64, 2, 2, 96, 128, 128], P('sess', None, None, None, 'band'), may hold values from -6 to 6
- holder_map: int32 [64], replicated, may hold values from 0 to 63, as said below
- counts: int32 [64], replicated, may hold values from 0 to 2
- active: int32 [64], replicated, may hold values 0 or 1
- weight_one: bfloat16 [96, 2592], replicated, may hold values from -0.125 to 0.125
- weight_two: bfloat16 [96, 2592], replicated, may hold values from -0.125 to 0.125
- gain_one: float32 [96], replicated, may hold values from 0.25 to 1.75
- gain_two: float32 [96], replicated, may hold values from 0.25 to 1.75
Outputs:
- block_out: bfloat16 [64, 96, 128, 128], P('sess', None, 'band')
The draws below stay inside these ranges and needn't reach their ends.
Inputs may be any that keep to these rules, and one draw needn't show every extreme that they name: holder_map is a permutation of 0 to 63; slot k lies at sess index k // 4; the cache slots of the 4 sessions of one sess index lie at 4 different sess indices: at most one of them at any one sess index.
All inputs are finite; a program needn't handle non-finite values.
Results may differ from the reference program's by a relative error of at most 0.0016.
Values may be sent and summed in bfloat16 or wider, within the bound.
No kernel may reach another device: no remote copies, remote signals or barrier semaphores. Data moves between devices by JAX's collectives and lax.ppermute only.
A program may use at most 64 MiB of HBM per device.

```python
import math
import jax
import jax.numpy as jnp
from jax import lax

C = 96
SESS_DEV = 4
WIDTH = 128
SESSIONS = 64
ROWS = 128
N_SESS = 16


def draw_holder_map(key, part):
    key = jax.random.fold_in(key, 11)
    first_key, second_key, third_key = jax.random.split(key, 3)
    session_ids = jnp.arange(SESSIONS, dtype=jnp.int32)
    owner = session_ids // SESS_DEV
    within = session_ids % SESS_DEV
    offsets = jax.random.permutation(first_key, SESS_DEV).astype(jnp.int32)
    relabel = jax.random.permutation(second_key, N_SESS).astype(jnp.int32)
    holder = relabel[(owner + offsets[within]) % N_SESS]
    tiebreak = jax.random.permutation(third_key, SESSIONS).astype(jnp.int32)
    score = holder * SESSIONS + tiebreak
    order = jnp.argsort(score, stable=True).astype(jnp.int32)
    slots = jnp.zeros((SESSIONS,), jnp.int32).at[order].set(session_ids)
    return slots


def draw_frame(key, part):
    key = jax.random.fold_in(key, 23)
    base_key, chan_key, pixel_key = jax.random.split(key, 3)
    shape_full = (SESSIONS, C, ROWS, WIDTH)
    base = jnp.clip(jax.random.normal(base_key, shape_full, jnp.float32), -4.0, 4.0)
    chan_scale = jnp.exp(jax.random.uniform(chan_key, (SESSIONS, C, 1, 1), jnp.float32, math.log(0.3), math.log(3.0)))
    pixel_scale = jnp.exp(jax.random.uniform(pixel_key, (SESSIONS, 1, ROWS, WIDTH), jnp.float32, math.log(0.3), math.log(3.0)))
    values = base * chan_scale * pixel_scale
    return values.astype(jnp.bfloat16)


def plant(array, key, low, largest):
    shape = array.shape
    index_at = [jax.random.randint(jax.random.fold_in(key, axis), (), 0, shape[axis]) for axis in range(len(shape))]
    array = array.at[tuple(index_at)].set(low)
    longest = shape.index(max(shape))
    index_at[longest] = (index_at[longest] + 1) % shape[longest]
    return array.at[tuple(index_at)].set(largest)


def shard_levels(key, shape, cuts, smallest, largest):
    gain, own = 1.0, jax.random.fold_in(key, 6)
    for dim, parts in cuts:
        steps = jnp.exp(jax.random.uniform(jax.random.fold_in(own, dim), (parts,), jnp.float32, smallest / len(cuts), largest / len(cuts)))
        gain = gain * jnp.repeat(steps, shape[dim] // parts).reshape([-1 if axis == dim else 1 for axis in range(len(shape))])
    return gain


def noise(key, shape, deviation, bound, cuts=(), kind=jnp.bfloat16):
    result = jax.random.normal(key, shape, jnp.float32) * deviation
    if len(cuts) > 0:
        result = shard_levels(key, shape, cuts, -0.22, 0.18) * result
    return jnp.clip(result, min=-bound, max=bound).astype(kind)


def setup_inputs(seed: int = 0) -> dict:
    key_of = jax.random.split(jax.random.key(seed), 10)
    frame = draw_frame(jax.random.fold_in(key_of[9], 71), 0)
    cache = noise(key_of[1], (SESSIONS, 2, 2, C, ROWS, WIDTH), 1.0, 6.0, ((0, 16), (4, 32)))
    holder_map = draw_holder_map(jax.random.fold_in(key_of[9], 71), 0)
    counts = plant(jax.random.randint(key_of[3], (SESSIONS,), 0, 3), jax.random.fold_in(key_of[3], 1), 0, 2).astype(jnp.int32)
    active = plant((jax.random.randint(key_of[4], (SESSIONS,), 0, 4) < 3).astype(jnp.int32), jax.random.fold_in(key_of[4], 1), 0, 1)
    weight_one = noise(key_of[5], (C, 27 * C), (27 * C) ** -0.5, 0.125)
    weight_two = noise(key_of[6], (C, 27 * C), (27 * C) ** -0.5, 0.125)
    gain_one = jnp.clip(1.0 + 0.15 * jax.random.normal(key_of[7], (C,), jnp.float32), 0.25, 1.75)
    gain_two = jnp.clip(1.0 + 0.15 * jax.random.normal(key_of[8], (C,), jnp.float32), 0.25, 1.75)
    return {"frame": frame, "cache": cache, "holder_map": holder_map, "counts": counts, "active": active, "weight_one": weight_one, "weight_two": weight_two, "gain_one": gain_one, "gain_two": gain_two}


def norm_silu(values, gain_vec):
    mean_square = lax.optimization_barrier(jnp.mean(values * values, axis=0, keepdims=True))
    scaled = values * lax.rsqrt(mean_square + 1e-06) * gain_vec[:, None, None]
    return jax.nn.silu(scaled)

def conv_frame(frames_stack, weight):
    channels = frames_stack.shape[1]
    padded = jnp.pad(frames_stack, ((0, 0), (0, 0), (1, 1), (1, 1)))
    accum_out = jnp.zeros((channels, ROWS, WIDTH), jnp.float32)
    for row_tap in range(3):
        pieces = [padded[time_tap, :, row_tap:row_tap + ROWS, col_tap:col_tap + WIDTH] for time_tap in range(3) for col_tap in range(3)]
        columns = jnp.concatenate(pieces, axis=0).astype(jnp.float32)
        weight_block = weight[:, row_tap * 9 * channels:(row_tap + 1) * 9 * channels].astype(jnp.float32)
        accum_out = accum_out + jnp.einsum('ok,krw->orw', weight_block, columns, precision=lax.Precision.HIGHEST)
    return accum_out

def reference(frame, cache, holder_map, counts, active, weight_one, weight_two, gain_one, gain_two):

    def one_session(index):
        current = frame[index]
        slabs = lax.dynamic_index_in_dim(cache, holder_map[index], 0, keepdims=False)
        live = jnp.arange(2, dtype=jnp.int32) >= 2 - counts[index]
        slabs = jnp.where(live[None, :, None, None, None], slabs, jnp.zeros_like(slabs))
        act_one = norm_silu(current.astype(jnp.float32), gain_one).astype(jnp.bfloat16)
        hidden_one = conv_frame(jnp.concatenate([slabs[0], act_one[None]], axis=0), weight_one)
        act_two = norm_silu(hidden_one, gain_two).astype(jnp.bfloat16)
        hidden_two = conv_frame(jnp.concatenate([slabs[1], act_two[None]], axis=0), weight_two)
        active_scale = active[index].astype(jnp.float32)
        return (active_scale * (current.astype(jnp.float32) + hidden_two)).astype(jnp.bfloat16)
    return lax.map(one_session, jnp.arange(SESSIONS, dtype=jnp.int32))
```

```python
import jax
import jax.numpy as jnp
from jax import lax
from jax.experimental import pallas as pl
from jax.experimental.pallas import tpu as pltpu
from jax.sharding import PartitionSpec as P

F32 = jnp.float32
BF16 = jnp.bfloat16


def three_taps(values):
    width = values.shape[1]
    column = lax.broadcasted_iota(jnp.int32, values.shape, 1)
    before = jnp.where(column == 0, 0.0, pltpu.roll(values, 1, 1))
    after = jnp.where(column == width - 1, 0.0, pltpu.roll(values, width - 1, 1))
    return before.astype(BF16), values.astype(BF16), after.astype(BF16)


def store_taps(cols_ref, at, channels, half, values):
    width = values.shape[1]
    for tap, moved in enumerate(three_taps(values)):
        cols_ref[at + tap * channels : at + (tap + 1) * channels, half * width : (half + 1) * width] = moved


def norm_silu(values, gain):
    mean_square = jnp.mean(values * values, axis=0, keepdims=True)
    scaled = values * lax.rsqrt(mean_square + 1e-06) * gain
    return scaled / (1.0 + jnp.exp(-scaled))


def past_kernel(live_ref, own_ref, above_ref, below_ref, w_one_ref, w_two_ref, one_ref, two_ref, cols_ref):
    pair = pl.program_id(0)
    rows, channels = own_ref.shape[3], own_ref.shape[4]
    step = 2 * 3 * channels

    def fill(slot, half, frame, source):
        keep = live_ref[2 * (2 * pair + half) + frame]
        values = source.astype(F32) * keep.astype(F32)
        store_taps(cols_ref, slot * step + frame * 3 * channels, channels, half, values)

    for half in range(2):
        for frame in range(2):
            for slot in range(rows + 4):
                if slot < 2:
                    source = above_ref[half, frame, slot]
                elif slot < rows + 2:
                    source = own_ref[0, half, frame, slot - 2]
                else:
                    source = below_ref[half, frame, slot - rows - 2]
                fill(slot, half, frame, source)
    for row in range(rows + 2):
        one_ref[0, row] = jnp.dot(w_one_ref[...], cols_ref[row * step : (row + 3) * step, :], preferred_element_type=F32)
    for half in range(2):
        for frame in range(2):
            for slot in range(rows + 2):
                if slot < 1:
                    source = above_ref[half, frame, 2]
                elif slot < rows + 1:
                    source = own_ref[1, half, frame, slot - 1]
                else:
                    source = below_ref[half, frame, 2]
                fill(slot, half, frame, source)
    for row in range(rows):
        two_ref[0, row] = jnp.dot(w_two_ref[...], cols_ref[row * step : (row + 3) * step, :], preferred_element_type=F32)


def past_sums(live, own, above, below, w_one, w_two):
    _, sessions, frames, rows, channels, width = own.shape
    pairs = sessions // 2
    whole = lambda p, live: (0, 0)
    return pl.pallas_call(
        past_kernel,
        grid_spec=pltpu.PrefetchScalarGridSpec(
            num_scalar_prefetch=1,
            grid=(pairs,),
            in_specs=[
                pl.BlockSpec((2, 2, frames, rows, channels, width), lambda p, live: (0, p, 0, 0, 0, 0)),
                pl.BlockSpec((2, frames, 3, channels, width), lambda p, live: (p, 0, 0, 0, 0)),
                pl.BlockSpec((2, frames, 3, channels, width), lambda p, live: (p, 0, 0, 0, 0)),
                pl.BlockSpec(w_one.shape, whole),
                pl.BlockSpec(w_two.shape, whole),
            ],
            out_specs=[
                pl.BlockSpec((1, rows + 2, channels, 2 * width), lambda p, live: (p, 0, 0, 0)),
                pl.BlockSpec((1, rows, channels, 2 * width), lambda p, live: (p, 0, 0, 0)),
            ],
            scratch_shapes=[pltpu.VMEM(((rows + 4) * 6 * channels, 2 * width), BF16)],
        ),
        out_shape=[
            jax.ShapeDtypeStruct((pairs, rows + 2, channels, 2 * width), F32),
            jax.ShapeDtypeStruct((pairs, rows, channels, 2 * width), F32),
        ],
        compiler_params=pltpu.CompilerParams(vmem_limit_bytes=40 * 1024 * 1024),
        cost_estimate=pl.CostEstimate(flops=4 * 10**9, bytes_accessed=6 * 10**6, transcendentals=0),
        name="past_sums",
    )(live, own, above, below, w_one, w_two)


def act_kernel(flags_ref, own_ref, above_ref, below_ref, one_ref, two_ref, w_one_ref, w_two_ref, g_one_ref, g_two_ref, out_ref, cols_ref):
    pair = pl.program_id(0)
    channels, width = w_one_ref.shape[0], own_ref.shape[3]
    part = own_ref.shape[2]
    parts = channels // part
    rows = own_ref.shape[0] // parts
    step = 3 * channels

    def frame_row(ref, row, half):
        return jnp.concatenate([ref[row * parts + q, half].astype(F32) for q in range(parts)], axis=0)

    g_one, g_two = g_one_ref[...], g_two_ref[...]
    for half in range(2):
        for slot in range(rows + 4):
            if slot < 2:
                values = frame_row(above_ref, slot, half)
            elif slot < rows + 2:
                values = frame_row(own_ref, slot - 2, half)
            else:
                values = frame_row(below_ref, slot - rows - 2, half)
            store_taps(cols_ref, slot * step, channels, half, norm_silu(values, g_one))
    acts = []
    for row in range(rows + 2):
        hidden = one_ref[0, row] + jnp.dot(
            w_one_ref[...], cols_ref[row * step : (row + 3) * step, :], preferred_element_type=F32
        )
        act = norm_silu(hidden, g_two)
        if row == 0:
            act = act * flags_ref[0].astype(F32)
        elif row == rows + 1:
            act = act * flags_ref[1].astype(F32)
        base = (rows + 4) * step + row * step
        for half in range(2):
            store_taps(cols_ref, base, channels, half, act[:, half * width : (half + 1) * width])
    for row in range(rows):
        base = (rows + 4) * step + row * step
        hidden = two_ref[0, row] + jnp.dot(
            w_two_ref[...], cols_ref[base : base + 3 * step, :], preferred_element_type=F32
        )
        for half in range(2):
            active = flags_ref[2 + 2 * pair + half].astype(F32)
            total = active * (frame_row(own_ref, row, half) + hidden[:, half * width : (half + 1) * width])
            for q in range(parts):
                out_ref[row * parts + q, half] = total[q * part : (q + 1) * part].astype(BF16)


def act_block(flags, own, above, below, one, two, w_one, w_two, g_one, g_two):
    pieces, sessions, part, width = own.shape
    pairs, rows, channels, _ = two.shape
    whole = lambda p, flags: (0, 0)
    piece_block = lambda count: pl.BlockSpec((count, 2, part, width), lambda p, flags: (0, p, 0, 0))
    return pl.pallas_call(
        act_kernel,
        grid_spec=pltpu.PrefetchScalarGridSpec(
            num_scalar_prefetch=1,
            grid=(pairs,),
            in_specs=[
                piece_block(pieces),
                piece_block(above.shape[0]),
                piece_block(below.shape[0]),
                pl.BlockSpec((1,) + one.shape[1:], lambda p, flags: (p, 0, 0, 0)),
                pl.BlockSpec((1,) + two.shape[1:], lambda p, flags: (p, 0, 0, 0)),
                pl.BlockSpec(w_one.shape, whole),
                pl.BlockSpec(w_two.shape, whole),
                pl.BlockSpec(g_one.shape, whole),
                pl.BlockSpec(g_two.shape, whole),
            ],
            out_specs=piece_block(pieces),
            scratch_shapes=[pltpu.VMEM(((2 * rows + 6) * 3 * channels, 2 * width), BF16)],
        ),
        out_shape=jax.ShapeDtypeStruct(own.shape, BF16),
        compiler_params=pltpu.CompilerParams(vmem_limit_bytes=40 * 1024 * 1024),
        cost_estimate=pl.CostEstimate(flops=2 * 10**9, bytes_accessed=4 * 10**6, transcendentals=10**6),
        name="act_block",
    )(flags, own, above, below, one, two, w_one, w_two, g_one, g_two)


def scatter_kernel(map_ref, in_ref, out_ref):
    def body(i, carry):
        out_ref[map_ref[i]] = in_ref[i]
        return carry

    lax.fori_loop(0, in_ref.shape[0], body, 0, unroll=8)


def gather_kernel(map_ref, in_ref, out_ref):
    def body(i, carry):
        out_ref[i] = in_ref[map_ref[i]]
        return carry

    lax.fori_loop(0, in_ref.shape[0], body, 0, unroll=8)


def reorder(kernel, slots, pieces, name):
    spec = pl.BlockSpec(pieces.shape, lambda i, slots: (0, 0, 0))
    return pl.pallas_call(
        kernel,
        grid_spec=pltpu.PrefetchScalarGridSpec(num_scalar_prefetch=1, grid=(1,), in_specs=[spec], out_specs=spec),
        out_shape=jax.ShapeDtypeStruct(pieces.shape, pieces.dtype),
        name=name,
    )(slots, pieces)


def exchange(pieces):
    return lax.all_to_all(pieces, "sess", 0, 0, tiled=True)


def local(frame, cache, holder_map, counts, active, weight_one, weight_two, gain_one, gain_two):
    sess_count, band_count = lax.axis_size("sess"), lax.axis_size("band")
    me, band = lax.axis_index("sess"), lax.axis_index("band")
    sessions, channels, rows, width = frame.shape
    parts = sess_count // rows
    part = channels // parts
    down = [(i, i + 1) for i in range(band_count - 1)]
    up = [(i + 1, i) for i in range(band_count - 1)]

    my_slots = me * sessions + jnp.arange(sessions, dtype=jnp.int32)
    here = holder_map[None, :] == my_slots[:, None]
    my_counts = jnp.sum(jnp.where(here, counts[None, :], 0), axis=1)
    my_active = jnp.sum(jnp.where(here, active[None, :], 0), axis=1)
    live = (jnp.arange(2, dtype=jnp.int32)[None, :] >= 2 - my_counts[:, None]).astype(jnp.int32).reshape(-1)
    flags = jnp.concatenate([jnp.stack([band > 0, band < band_count - 1]).astype(jnp.int32), my_active])

    cut = frame.reshape(sessions, parts, part, rows, width).transpose(3, 1, 0, 2, 4)
    spread = exchange(cut.reshape(sess_count, sessions, part, width))

    own = cache.transpose(1, 0, 2, 4, 3, 5)
    above = lax.ppermute(jnp.concatenate([own[0, :, :, rows - 2 :], own[1, :, :, rows - 1 :]], axis=2), "band", down)
    below = lax.ppermute(jnp.concatenate([own[0, :, :, :2], own[1, :, :, :1]], axis=2), "band", up)
    w_one = weight_one.reshape(channels, 3, 3, 3 * channels)
    w_two = weight_two.reshape(channels, 3, 3, 3 * channels)
    past_w = lambda w: w[:, :, :2].reshape(channels, -1)
    new_w = lambda w: w[:, :, 2].reshape(channels, -1)
    one, two = past_sums(live, own, above, below, past_w(w_one), past_w(w_two))

    sorted_pieces = reorder(scatter_kernel, holder_map, spread.reshape(-1, part, width), "to_holders")
    held = exchange(sorted_pieces.reshape(sess_count, sessions, part, width))
    half = sess_count - 2 * parts
    held_above = lax.ppermute(held[half:], "band", down)
    held_below = lax.ppermute(held[: 2 * parts], "band", up)
    result = act_block(
        flags, held, held_above, held_below, one, two, new_w(w_one), new_w(w_two), gain_one[:, None], gain_two[:, None]
    )

    spread_result = exchange(result)
    home_pieces = reorder(gather_kernel, holder_map, spread_result.reshape(-1, part, width), "to_homes")
    home = exchange(home_pieces.reshape(sess_count, sessions, part, width))
    home = home.reshape(rows, parts, sessions, part, width).transpose(2, 1, 3, 0, 4)
    return home.reshape(sessions, channels, rows, width)


def solution(mesh):
    return jax.shard_map(
        local,
        mesh=mesh,
        in_specs=(
            P("sess", None, "band", None),
            P("sess", None, None, None, "band", None),
            P(),
            P(),
            P(),
            P(),
            P(),
            P(),
            P(),
        ),
        out_specs=P("sess", None, "band", None),
        check_vma=False,
    )
```

```python
import functools

import jax
import jax.numpy as jnp
from jax import lax
from jax.experimental import pallas as pl
from jax.experimental.pallas import tpu as pltpu
from jax.sharding import PartitionSpec as P

F32 = jnp.float32
BF16 = jnp.bfloat16


def three_taps(values):
    width = values.shape[1]
    column = lax.broadcasted_iota(jnp.int32, values.shape, 1)
    before = jnp.where(column == 0, 0.0, pltpu.roll(values, 1, 1))
    after = jnp.where(column == width - 1, 0.0, pltpu.roll(values, width - 1, 1))
    return before.astype(BF16), values.astype(BF16), after.astype(BF16)


def store_taps(cols_ref, at, channels, half, values):
    width = values.shape[1]
    for tap, moved in enumerate(three_taps(values)):
        cols_ref[at + tap * channels : at + (tap + 1) * channels, half * width : (half + 1) * width] = moved


def norm_silu(values, gain):
    mean_square = jnp.mean(values * values, axis=0, keepdims=True)
    scaled = values * lax.rsqrt(mean_square + 1e-06) * gain
    return 0.5 * scaled * (1.0 + jnp.tanh(0.5 * scaled))


def past_kernel(place_ref, session_of_ref, counts_ref, own_ref, above_ref, below_ref, w_one_ref, w_two_ref, one_hbm, two_hbm, one_cols_ref, two_cols_ref, one_ref, two_ref, sems):
    _, rows, sessions, frames, channels, _ = own_ref.shape
    step = frames * 3 * channels
    copies = []
    for pair in range(sessions // 2):
        for half in range(2):
            session = 2 * pair + half
            count = counts_ref[session_of_ref[place_ref[0] * sessions + session]]
            for frame in range(frames):
                live = (frame >= 2 - count).astype(F32)
                one_rows = [above_ref.at[0], above_ref.at[1]] + [own_ref.at[0, r] for r in range(rows)] + [below_ref.at[0], below_ref.at[1]]
                two_rows = [above_ref.at[2]] + [own_ref.at[1, r] for r in range(rows)] + [below_ref.at[2]]
                for cols_ref, row_refs in ((one_cols_ref, one_rows), (two_cols_ref, two_rows)):
                    for slot, row_ref in enumerate(row_refs):
                        values = row_ref[session, frame].astype(F32) * live
                        store_taps(cols_ref.at[pair], slot * step + frame * 3 * channels, channels, half, values)
        for i, (out_hbm, out_ref, w_ref, cols_ref) in enumerate(
            ((one_hbm, one_ref, w_one_ref, one_cols_ref), (two_hbm, two_ref, w_two_ref, two_cols_ref))
        ):
            for row in range(out_ref.shape[1]):
                out_ref[pair, row] = jnp.dot(
                    w_ref[...], cols_ref[pair, row * step : (row + 3) * step, :], preferred_element_type=F32
                )
            copies.append(pltpu.make_async_copy(out_ref.at[pair], out_hbm.at[pair], sems.at[pair, i]))
            copies[-1].start()
    for copy in copies:
        copy.wait()


def past_sums(place, session_of, counts, own, above, below, w_one, w_two):
    _, rows, sessions, frames, channels, width = own.shape
    pairs, lanes, step = sessions // 2, 2 * width, frames * 3 * channels
    vmem, smem = pl.BlockSpec(memory_space=pltpu.VMEM), pl.BlockSpec(memory_space=pltpu.SMEM)
    return pl.pallas_call(
        past_kernel,
        in_specs=[smem, smem, smem, vmem, vmem, vmem, vmem, vmem],
        out_specs=[pl.BlockSpec(memory_space=pltpu.HBM)] * 2,
        out_shape=[
            pltpu.HBM((pairs, rows + 2, channels, lanes), F32),
            pltpu.HBM((pairs, rows, channels, lanes), F32),
        ],
        scratch_shapes=[
            pltpu.VMEM((pairs, (rows + 4) * step, lanes), BF16),
            pltpu.VMEM((pairs, (rows + 2) * step, lanes), BF16),
            pltpu.VMEM((pairs, rows + 2, channels, lanes), F32),
            pltpu.VMEM((pairs, rows, channels, lanes), F32),
            pltpu.SemaphoreType.DMA((pairs, 2)),
        ],
        compiler_params=pltpu.CompilerParams(vmem_limit_bytes=24 * 1024 * 1024),
        cost_estimate=pl.CostEstimate(flops=4 * 10**9, bytes_accessed=6 * 10**6, transcendentals=0),
        name="past_sums",
    )(place, session_of, counts, own, above, below, w_one, w_two)


def act_kernel(place_ref, session_of_ref, active_ref, own_ref, above_ref, below_ref, one_hbm, two_hbm, w_one_hbm, w_two_hbm, g_one_ref, g_two_ref, out_ref, cols_ref, acts_ref, one_ref, two_ref, w_one_ref, w_two_ref, sems, *, bands):
    channels, width = w_one_hbm.shape[0], own_ref.shape[3]
    sessions, part = own_ref.shape[1], own_ref.shape[2]
    parts = channels // part
    rows = own_ref.shape[0] // parts
    step = 3 * channels
    copies = [
        pltpu.make_async_copy(source, target, sems.at[i])
        for i, (source, target) in enumerate(
            ((w_one_hbm, w_one_ref), (one_hbm, one_ref), (w_two_hbm, w_two_ref), (two_hbm, two_ref))
        )
    ]
    for copy in copies:
        copy.start()
    first = (place_ref[1] > 0).astype(F32)
    last = (place_ref[1] < bands - 1).astype(F32)

    def frame_row(ref, row, session):
        return jnp.concatenate([ref[row * parts + q, session].astype(F32) for q in range(parts)], axis=0)

    g_one, g_two = g_one_ref[...], g_two_ref[...]
    for pair in range(sessions // 2):
        for slot in range(rows + 4):
            for half in range(2):
                if slot < 2:
                    values = frame_row(above_ref, slot, 2 * pair + half)
                elif slot < rows + 2:
                    values = frame_row(own_ref, slot - 2, 2 * pair + half)
                else:
                    values = frame_row(below_ref, slot - rows - 2, 2 * pair + half)
                store_taps(cols_ref.at[pair], slot * step, channels, half, norm_silu(values, g_one))
        if pair == 0:
            copies[0].wait()
            copies[1].wait()
        for row in range(rows + 2):
            hidden = one_ref[pair, row] + jnp.dot(
                w_one_ref[...], cols_ref[pair, row * step : (row + 3) * step, :], preferred_element_type=F32
            )
            act = norm_silu(hidden, g_two)
            if row == 0:
                act = act * first
            elif row == rows + 1:
                act = act * last
            for half in range(2):
                store_taps(acts_ref.at[pair], row * step, channels, half, act[:, half * width : (half + 1) * width])
        if pair == 0:
            copies[2].wait()
            copies[3].wait()
        for row in range(rows):
            hidden = two_ref[pair, row] + jnp.dot(
                w_two_ref[...], acts_ref[pair, row * step : (row + 3) * step, :], preferred_element_type=F32
            )
            for half in range(2):
                session = 2 * pair + half
                active = active_ref[session_of_ref[place_ref[0] * sessions + session]].astype(F32)
                total = active * (frame_row(own_ref, row, session) + hidden[:, half * width : (half + 1) * width])
                for q in range(parts):
                    out_ref[row * parts + q, session] = total[q * part : (q + 1) * part].astype(BF16)


def act_block(bands, place, session_of, active, own, above, below, one, two, w_one, w_two, g_one, g_two):
    pairs, rows, channels, lanes = two.shape
    step = 3 * channels
    one, two, w_one, w_two = (pltpu.with_memory_space_constraint(x, pltpu.HBM) for x in (one, two, w_one, w_two))
    vmem, smem = pl.BlockSpec(memory_space=pltpu.VMEM), pl.BlockSpec(memory_space=pltpu.SMEM)
    return pl.pallas_call(
        functools.partial(act_kernel, bands=bands),
        in_specs=[smem] * 3 + [vmem] * 3 + [pl.BlockSpec(memory_space=pltpu.HBM)] * 4 + [vmem] * 2,
        out_specs=vmem,
        out_shape=jax.ShapeDtypeStruct(own.shape, BF16),
        scratch_shapes=[
            pltpu.VMEM((pairs, (rows + 4) * step, lanes), BF16),
            pltpu.VMEM((pairs, (rows + 2) * step, lanes), BF16),
            pltpu.VMEM(one.shape, F32),
            pltpu.VMEM(two.shape, F32),
            pltpu.VMEM(w_one.shape, BF16),
            pltpu.VMEM(w_two.shape, BF16),
            pltpu.SemaphoreType.DMA((4,)),
        ],
        compiler_params=pltpu.CompilerParams(vmem_limit_bytes=20 * 1024 * 1024),
        cost_estimate=pl.CostEstimate(flops=2 * 10**9, bytes_accessed=4 * 10**6, transcendentals=10**6),
        name="act_block",
    )(place, session_of, active, own, above, below, one, two, w_one, w_two, g_one, g_two)


def weights_kernel(one_ref, two_ref, past_one_ref, past_two_ref, new_one_ref, new_two_ref):
    third = one_ref.shape[1] // 3
    new = third // 3
    past = third - new
    for source, past_out, new_out in ((one_ref, past_one_ref, new_one_ref), (two_ref, past_two_ref, new_two_ref)):
        values = source[...]
        rows = [values[:, dy * third : (dy + 1) * third] for dy in range(3)]
        past_out[...] = jnp.concatenate([row[:, :past] for row in rows], axis=1)
        new_out[...] = jnp.concatenate([row[:, past:] for row in rows], axis=1)


def split_weights(one, two):
    channels, columns = one.shape
    past = jax.ShapeDtypeStruct((channels, columns // 3 * 2), one.dtype)
    new = jax.ShapeDtypeStruct((channels, columns // 3), one.dtype)
    return pl.pallas_call(
        weights_kernel,
        out_shape=[past, past, new, new],
        compiler_params=pltpu.CompilerParams(vmem_limit_bytes=16 * 1024 * 1024),
        cost_estimate=pl.CostEstimate(flops=0, bytes_accessed=2 * 10**6, transcendentals=0),
        name="split_weights",
    )(one, two)


def take_slots(pieces, slots):
    return lax.gather(
        pieces,
        slots[:, None],
        lax.GatherDimensionNumbers(offset_dims=(1, 2), collapsed_slice_dims=(0,), start_index_map=(0,)),
        slice_sizes=(1,) + pieces.shape[1:],
        unique_indices=True,
        mode=lax.GatherScatterMode.CLIP,
    )


def take_kernel(slots_ref, in_ref, out_ref):
    for slot in range(in_ref.shape[0]):
        out_ref[slot] = in_ref[slots_ref[slot]]


def take_in_vmem(pieces, slots):
    vmem = pl.BlockSpec(memory_space=pltpu.VMEM)
    return pl.pallas_call(
        take_kernel,
        in_specs=[pl.BlockSpec(memory_space=pltpu.SMEM), vmem],
        out_specs=vmem,
        out_shape=jax.ShapeDtypeStruct(pieces.shape, pieces.dtype),
        compiler_params=pltpu.CompilerParams(vmem_limit_bytes=4 * 1024 * 1024),
        name="take_in_vmem",
    )(slots, pieces)


def exchange(pieces):
    return lax.all_to_all(pieces, "sess", 0, 0, tiled=True)


def local(frame, cache, holder_map, counts, active, weight_one, weight_two, gain_one, gain_two):
    sess_count, band_count = lax.axis_size("sess"), lax.axis_size("band")
    me, band = lax.axis_index("sess"), lax.axis_index("band")
    sessions, channels, rows, width = frame.shape
    parts = sess_count // rows
    part = channels // parts
    down = [(i, i + 1) for i in range(band_count - 1)]
    up = [(i + 1, i) for i in range(band_count - 1)]

    ids = jnp.arange(sess_count * sessions, dtype=jnp.int32)
    session_of = jnp.sum(jnp.where(holder_map[None, :] == ids[:, None], ids[None, :], 0), axis=1)
    place = jnp.stack([me, band]).astype(jnp.int32)

    cut = frame.reshape(sessions, parts, part, rows, width).transpose(3, 1, 0, 2, 4)
    cut, cache = lax.optimization_barrier((cut, cache))
    spread = exchange(cut.reshape(sess_count, sessions, part, width))

    own = cache.transpose(1, 4, 0, 2, 3, 5)
    above = lax.ppermute(jnp.concatenate([own[0, rows - 2 :], own[1, rows - 1 :]]), "band", down)
    below = lax.ppermute(jnp.concatenate([own[0, :2], own[1, :1]]), "band", up)
    past_one, past_two, new_one, new_two = split_weights(weight_one, weight_two)
    one, two = past_sums(place, session_of, counts, own, above, below, past_one, past_two)

    sorted_pieces = take_slots(spread.reshape(-1, part, width), session_of)
    held = exchange(sorted_pieces.reshape(sess_count, sessions, part, width))
    held, one, two = lax.optimization_barrier((held, one, two))
    half = sess_count - 2 * parts
    held_above = lax.ppermute(held[half:], "band", down)
    held_below = lax.ppermute(held[: 2 * parts], "band", up)
    result = act_block(
        band_count, place, session_of, active, held, held_above, held_below,
        one, two, new_one, new_two, gain_one[:, None], gain_two[:, None],
    )

    spread_result = exchange(result)
    home_pieces = take_in_vmem(spread_result.reshape(-1, part, width), holder_map)
    home = exchange(home_pieces.reshape(sess_count, sessions, part, width))
    home = home.reshape(rows, parts, sessions, part, width).transpose(2, 1, 3, 0, 4)
    return home.reshape(sessions, channels, rows, width)


def solution(mesh):
    return jax.shard_map(
        local,
        mesh=mesh,
        in_specs=(
            P("sess", None, "band", None),
            P("sess", None, None, None, "band", None),
            P(),
            P(),
            P(),
            P(),
            P(),
            P(),
            P(),
        ),
        out_specs=P("sess", None, "band", None),
        check_vma=False,
    )
```

```python
import functools

import jax
import jax.numpy as jnp
from jax import lax
from jax.experimental import pallas as pl
from jax.experimental.pallas import tpu as pltpu
from jax.sharding import PartitionSpec as P

F32 = jnp.float32
BF16 = jnp.bfloat16


def three_taps(values):
    width = values.shape[1]
    column = lax.broadcasted_iota(jnp.int32, values.shape, 1)
    before = jnp.where(column == 0, 0.0, pltpu.roll(values, 1, 1))
    after = jnp.where(column == width - 1, 0.0, pltpu.roll(values, width - 1, 1))
    return before.astype(BF16), values.astype(BF16), after.astype(BF16)


def store_taps(cols_ref, at, channels, half, values):
    width = values.shape[1]
    for tap, moved in enumerate(three_taps(values)):
        cols_ref[at + tap * channels : at + (tap + 1) * channels, half * width : (half + 1) * width] = moved


def norm_silu(values, gain):
    mean_square = jnp.mean(values * values, axis=0, keepdims=True)
    scaled = values * lax.rsqrt(mean_square + 1e-06) * gain
    return 0.5 * scaled * (1.0 + jnp.tanh(0.5 * scaled))


def past_kernel(place_ref, session_of_ref, counts_ref, own_ref, below_ref, above_ref, w_one_ref, w_two_ref, one_hbm, two_hbm, one_cols_ref, two_cols_ref, one_ref, two_ref, sems):
    _, rows, sessions, frames, channels, _ = own_ref.shape
    step = frames * 3 * channels
    copies = []
    for pair in range(sessions // 2):
        for half in range(2):
            session = 2 * pair + half
            count = counts_ref[session_of_ref[place_ref[0] * sessions + session]]
            for frame in range(frames):
                live = (frame >= 2 - count).astype(F32)
                one_rows = [above_ref.at[0], above_ref.at[1]] + [own_ref.at[0, r] for r in range(rows)] + [below_ref.at[0], below_ref.at[1]]
                two_rows = [above_ref.at[2]] + [own_ref.at[1, r] for r in range(rows)] + [below_ref.at[2]]
                for cols_ref, row_refs in ((one_cols_ref, one_rows), (two_cols_ref, two_rows)):
                    for slot, row_ref in enumerate(row_refs):
                        values = row_ref[session, frame].astype(F32) * live
                        store_taps(cols_ref.at[pair], slot * step + frame * 3 * channels, channels, half, values)
        for i, (out_hbm, out_ref, w_ref, cols_ref) in enumerate(
            ((one_hbm, one_ref, w_one_ref, one_cols_ref), (two_hbm, two_ref, w_two_ref, two_cols_ref))
        ):
            for row in range(out_ref.shape[1]):
                out_ref[pair, row] = jnp.dot(
                    w_ref[...], cols_ref[pair, row * step : (row + 3) * step, :], preferred_element_type=F32
                )
            copies.append(pltpu.make_async_copy(out_ref.at[pair], out_hbm.at[pair], sems.at[pair, i]))
            copies[-1].start()
    for copy in copies:
        copy.wait()


def past_sums(place, session_of, counts, own, above, below, w_one, w_two):
    _, rows, sessions, frames, channels, width = own.shape
    pairs, lanes, step = sessions // 2, 2 * width, frames * 3 * channels
    vmem, smem = pl.BlockSpec(memory_space=pltpu.VMEM), pl.BlockSpec(memory_space=pltpu.SMEM)
    return pl.pallas_call(
        past_kernel,
        in_specs=[smem, smem, smem, vmem, vmem, vmem, vmem, vmem],
        out_specs=[pl.BlockSpec(memory_space=pltpu.HBM)] * 2,
        out_shape=[
            pltpu.HBM((pairs, rows + 2, channels, lanes), F32),
            pltpu.HBM((pairs, rows, channels, lanes), F32),
        ],
        scratch_shapes=[
            pltpu.VMEM((pairs, (rows + 4) * step, lanes), BF16),
            pltpu.VMEM((pairs, (rows + 2) * step, lanes), BF16),
            pltpu.VMEM((pairs, rows + 2, channels, lanes), F32),
            pltpu.VMEM((pairs, rows, channels, lanes), F32),
            pltpu.SemaphoreType.DMA((pairs, 2)),
        ],
        compiler_params=pltpu.CompilerParams(vmem_limit_bytes=24 * 1024 * 1024),
        cost_estimate=pl.CostEstimate(flops=4 * 10**9, bytes_accessed=6 * 10**6, transcendentals=0),
        name="past_sums",
    )(place, session_of, counts, own, below, above, w_one, w_two)


def frame_row(ref, row, session, parts):
    return jnp.concatenate([ref[row * parts + q, session].astype(F32) for q in range(parts)], axis=0)


def store_act(cols_ref, pair, slot, act):
    channels, width = act.shape[0], act.shape[1] // 2
    for half in range(2):
        store_taps(cols_ref.at[pair], slot * 3 * channels, channels, half, act[:, half * width : (half + 1) * width])


def own_kernel(own_ref, one_hbm, two_hbm, w_one_hbm, w_two_hbm, g_one_ref, g_two_ref, cols_ref, acts_ref, one_ref, two_ref, w_one_ref, w_two_ref, sems):
    channels = w_one_hbm.shape[0]
    parts = channels // own_ref.shape[2]
    rows = own_ref.shape[0] // parts
    step = 3 * channels
    copies = [
        pltpu.make_async_copy(source, target, sems.at[i])
        for i, (source, target) in enumerate(
            ((w_one_hbm, w_one_ref), (one_hbm, one_ref), (two_hbm, two_ref), (w_two_hbm, w_two_ref))
        )
    ]
    for copy in copies:
        copy.start()
    g_one, g_two = g_one_ref[...], g_two_ref[...]
    pairs = own_ref.shape[1] // 2
    for pair in range(pairs):
        for row in range(rows):
            for half in range(2):
                act = norm_silu(frame_row(own_ref, row, 2 * pair + half, parts), g_one)
                store_taps(cols_ref.at[pair], row * step, channels, half, act)
    copies[0].wait()
    copies[1].wait()
    for pair in range(pairs):
        for row in range(rows - 2):
            hidden = one_ref[pair, row + 2] + jnp.dot(
                w_one_ref[...], cols_ref[pair, row * step : (row + 3) * step, :], preferred_element_type=F32
            )
            store_act(acts_ref, pair, row, norm_silu(hidden, g_two))
    copies[2].wait()
    copies[3].wait()


def own_rows(own, one, two, w_one, w_two, g_one, g_two):
    pairs, rows, channels, lanes = two.shape
    step = 3 * channels
    vmem, hbm = pl.BlockSpec(memory_space=pltpu.VMEM), pl.BlockSpec(memory_space=pltpu.HBM)
    one, two, w_one, w_two = (pltpu.with_memory_space_constraint(x, pltpu.HBM) for x in (one, two, w_one, w_two))
    return pl.pallas_call(
        own_kernel,
        in_specs=[vmem] + [hbm] * 4 + [vmem] * 2,
        out_specs=[vmem] * 6,
        out_shape=[
            jax.ShapeDtypeStruct((pairs, rows * step, lanes), BF16),
            jax.ShapeDtypeStruct((pairs, (rows - 2) * step, lanes), BF16),
            jax.ShapeDtypeStruct(one.shape, F32),
            jax.ShapeDtypeStruct(two.shape, F32),
            jax.ShapeDtypeStruct(w_one.shape, BF16),
            jax.ShapeDtypeStruct(w_two.shape, BF16),
        ],
        scratch_shapes=[pltpu.SemaphoreType.DMA((4,))],
        compiler_params=pltpu.CompilerParams(vmem_limit_bytes=16 * 1024 * 1024),
        cost_estimate=pl.CostEstimate(flops=10**9, bytes_accessed=4 * 10**6, transcendentals=10**6),
        name="own_rows",
    )(own, one, two, w_one, w_two, g_one, g_two)


def side_kernel(place_ref, session_of_ref, active_ref, halo_ref, own_ref, own_cols_ref, mid_acts_ref, one_ref, two_ref, w_one_ref, w_two_ref, g_one_ref, g_two_ref, *rest, top, bands):
    out_ref, cols_ref, acts_ref = rest[-3:]
    channels = w_one_ref.shape[0]
    sessions, part = own_ref.shape[1], own_ref.shape[2]
    width = own_ref.shape[3]
    parts = channels // part
    rows = own_ref.shape[0] // parts
    step = 3 * channels
    inside = ((place_ref[1] > 0) if top else (place_ref[1] < bands - 1)).astype(F32)
    g_one, g_two = g_one_ref[...], g_two_ref[...]
    halo_at, own_at = (0, 2) if top else (2, 0)
    for pair in range(sessions // 2):
        for row in range(2):
            for half in range(2):
                act = norm_silu(frame_row(halo_ref, row, 2 * pair + half, parts), g_one)
                store_taps(cols_ref.at[pair], (halo_at + row) * step, channels, half, act)
        from_row = 0 if top else rows - 2
        cols_ref[pair, own_at * step : (own_at + 2) * step, :] = own_cols_ref[pair, from_row * step : (from_row + 2) * step, :]
        acts_ref[pair, own_at * step : (own_at + 2) * step, :] = mid_acts_ref[pair]
    first = 0 if top else rows
    for pair in range(sessions // 2):
        for row in range(2):
            hidden = one_ref[pair, first + row] + jnp.dot(
                w_one_ref[...], cols_ref[pair, row * step : (row + 3) * step, :], preferred_element_type=F32
            )
            act = norm_silu(hidden, g_two)
            if row == (0 if top else 1):
                act = act * inside
            store_act(acts_ref, pair, halo_at + row, act)
    first = 0 if top else rows - 2
    for pair in range(sessions // 2):
        for row in range(2):
            hidden = two_ref[pair, first + row] + jnp.dot(
                w_two_ref[...], acts_ref[pair, row * step : (row + 3) * step, :], preferred_element_type=F32
            )
            for half in range(2):
                session = 2 * pair + half
                active = active_ref[session_of_ref[place_ref[0] * sessions + session]].astype(F32)
                total = active * (
                    frame_row(own_ref, first + row, session, parts) + hidden[:, half * width : (half + 1) * width]
                )
                for q in range(parts):
                    out_ref[(first + row) * parts + q, session] = total[q * part : (q + 1) * part].astype(BF16)


def side_rows(top, bands, place, session_of, active, halo, own, held, g_one, g_two, earlier=None):
    own_cols, mid_acts, one, two, w_one, w_two = held
    pairs, rows, channels, lanes = two.shape
    step = 3 * channels
    vmem, smem = pl.BlockSpec(memory_space=pltpu.VMEM), pl.BlockSpec(memory_space=pltpu.SMEM)
    operands = [place, session_of, active, halo, own, own_cols, mid_acts, one, two, w_one, w_two, g_one, g_two]
    operands += [] if earlier is None else [earlier]
    return pl.pallas_call(
        functools.partial(side_kernel, top=top, bands=bands),
        in_specs=[smem] * 3 + [vmem] * (len(operands) - 3),
        out_specs=vmem,
        out_shape=jax.ShapeDtypeStruct(own.shape, BF16),
        input_output_aliases={} if earlier is None else {len(operands) - 1: 0},
        scratch_shapes=[pltpu.VMEM((pairs, 4 * step, lanes), BF16), pltpu.VMEM((pairs, 4 * step, lanes), BF16)],
        compiler_params=pltpu.CompilerParams(vmem_limit_bytes=16 * 1024 * 1024),
        cost_estimate=pl.CostEstimate(flops=10**9, bytes_accessed=4 * 10**6, transcendentals=10**6),
        name="top_rows" if top else "bottom_rows",
    )(*operands)


def weights_kernel(one_ref, two_ref, past_one_ref, past_two_ref, new_one_ref, new_two_ref):
    third = one_ref.shape[1] // 3
    new = third // 3
    past = third - new
    for source, past_out, new_out in ((one_ref, past_one_ref, new_one_ref), (two_ref, past_two_ref, new_two_ref)):
        values = source[...]
        rows = [values[:, dy * third : (dy + 1) * third] for dy in range(3)]
        past_out[...] = jnp.concatenate([row[:, :past] for row in rows], axis=1)
        new_out[...] = jnp.concatenate([row[:, past:] for row in rows], axis=1)


def split_weights(one, two):
    channels, columns = one.shape
    past = jax.ShapeDtypeStruct((channels, columns // 3 * 2), one.dtype)
    new = jax.ShapeDtypeStruct((channels, columns // 3), one.dtype)
    return pl.pallas_call(
        weights_kernel,
        out_shape=[past, past, new, new],
        compiler_params=pltpu.CompilerParams(vmem_limit_bytes=16 * 1024 * 1024),
        cost_estimate=pl.CostEstimate(flops=0, bytes_accessed=2 * 10**6, transcendentals=0),
        name="split_weights",
    )(one, two)


def take_slots(pieces, slots):
    return lax.gather(
        pieces,
        slots[:, None],
        lax.GatherDimensionNumbers(offset_dims=(1, 2), collapsed_slice_dims=(0,), start_index_map=(0,)),
        slice_sizes=(1,) + pieces.shape[1:],
        unique_indices=True,
        mode=lax.GatherScatterMode.CLIP,
    )


def take_kernel(slots_ref, in_ref, out_ref):
    for slot in range(in_ref.shape[0]):
        out_ref[slot] = in_ref[slots_ref[slot]]


def take_in_vmem(pieces, slots):
    vmem = pl.BlockSpec(memory_space=pltpu.VMEM)
    return pl.pallas_call(
        take_kernel,
        in_specs=[pl.BlockSpec(memory_space=pltpu.SMEM), vmem],
        out_specs=vmem,
        out_shape=jax.ShapeDtypeStruct(pieces.shape, pieces.dtype),
        compiler_params=pltpu.CompilerParams(vmem_limit_bytes=4 * 1024 * 1024),
        name="take_in_vmem",
    )(slots, pieces)


def exchange(pieces):
    return lax.all_to_all(pieces, "sess", 0, 0, tiled=True)


def local(frame, cache, holder_map, counts, active, weight_one, weight_two, gain_one, gain_two):
    sess_count, band_count = lax.axis_size("sess"), lax.axis_size("band")
    me, band = lax.axis_index("sess"), lax.axis_index("band")
    sessions, channels, rows, width = frame.shape
    parts = sess_count // rows
    part = channels // parts
    down = [(i, i + 1) for i in range(band_count - 1)]
    up = [(i + 1, i) for i in range(band_count - 1)]

    ids = jnp.arange(sess_count * sessions, dtype=jnp.int32)
    session_of = jnp.sum(jnp.where(holder_map[None, :] == ids[:, None], ids[None, :], 0), axis=1)
    place = jnp.stack([me, band]).astype(jnp.int32)

    cut = frame.reshape(sessions, parts, part, rows, width).transpose(3, 1, 0, 2, 4)
    cut, cache = lax.optimization_barrier((cut, cache))
    spread = exchange(cut.reshape(sess_count, sessions, part, width))

    own = cache.transpose(1, 4, 0, 2, 3, 5)
    below = lax.ppermute(jnp.concatenate([own[0, :2], own[1, :1]]), "band", up)
    above = lax.ppermute(jnp.concatenate([own[0, rows - 2 :], own[1, rows - 1 :]]), "band", down)
    past_one, past_two, new_one, new_two = split_weights(weight_one, weight_two)
    one, two = past_sums(place, session_of, counts, own, above, below, past_one, past_two)

    sorted_pieces = take_slots(spread.reshape(-1, part, width), session_of)
    held = exchange(sorted_pieces.reshape(sess_count, sessions, part, width))
    held, one, two = lax.optimization_barrier((held, one, two))
    half = sess_count - 2 * parts
    held_above = lax.ppermute(held[half:], "band", down)
    held_below = lax.ppermute(held[: 2 * parts], "band", up)
    gains = gain_one[:, None], gain_two[:, None]
    inner = own_rows(held, one, two, new_one, new_two, *gains)
    upper = side_rows(True, band_count, place, session_of, active, held_above, held, inner, *gains)
    result = side_rows(False, band_count, place, session_of, active, held_below, held, inner, *gains, earlier=upper)

    spread_result = exchange(result)
    home_pieces = take_in_vmem(spread_result.reshape(-1, part, width), holder_map)
    home = exchange(home_pieces.reshape(sess_count, sessions, part, width))
    home = home.reshape(rows, parts, sessions, part, width).transpose(2, 1, 3, 0, 4)
    return home.reshape(sessions, channels, rows, width)


def solution(mesh):
    return jax.shard_map(
        local,
        mesh=mesh,
        in_specs=(
            P("sess", None, "band", None),
            P("sess", None, None, None, "band", None),
            P(),
            P(),
            P(),
            P(),
            P(),
            P(),
            P(),
        ),
        out_specs=P("sess", None, "band", None),
        check_vma=False,
    )
```

```python
import functools

import jax
import jax.numpy as jnp
from jax import lax
from jax.experimental import pallas as pl
from jax.experimental.pallas import tpu as pltpu
from jax.sharding import PartitionSpec as P

F32 = jnp.float32
BF16 = jnp.bfloat16


def three_taps(values):
    width = values.shape[1]
    column = lax.broadcasted_iota(jnp.int32, values.shape, 1)
    before = jnp.where(column == 0, 0.0, pltpu.roll(values, 1, 1))
    after = jnp.where(column == width - 1, 0.0, pltpu.roll(values, width - 1, 1))
    return before.astype(BF16), values.astype(BF16), after.astype(BF16)


def store_taps(cols_ref, at, channels, half, values):
    width = values.shape[1]
    for tap, moved in enumerate(three_taps(values)):
        cols_ref[at + tap * channels : at + (tap + 1) * channels, half * width : (half + 1) * width] = moved


def norm_silu(values, gain):
    mean_square = jnp.mean(values * values, axis=0, keepdims=True)
    scaled = values * lax.rsqrt(mean_square + 1e-06) * gain
    return 0.5 * scaled * (1.0 + jnp.tanh(0.5 * scaled))


def past_kernel(place_ref, session_of_ref, counts_ref, own_ref, below_ref, above_ref, w_one_ref, w_two_ref, one_hbm, two_hbm, one_cols_ref, two_cols_ref, one_ref, two_ref, sems):
    _, rows, sessions, frames, channels, _ = own_ref.shape
    step = frames * 3 * channels
    copies = []
    for pair in range(sessions // 2):
        for half in range(2):
            session = 2 * pair + half
            count = counts_ref[session_of_ref[place_ref[0] * sessions + session]]
            for frame in range(frames):
                live = (frame >= 2 - count).astype(F32)
                one_rows = [above_ref.at[0], above_ref.at[1]] + [own_ref.at[0, r] for r in range(rows)] + [below_ref.at[0], below_ref.at[1]]
                two_rows = [above_ref.at[2]] + [own_ref.at[1, r] for r in range(rows)] + [below_ref.at[2]]
                for cols_ref, row_refs in ((one_cols_ref, one_rows), (two_cols_ref, two_rows)):
                    for slot, row_ref in enumerate(row_refs):
                        values = row_ref[session, frame].astype(F32) * live
                        store_taps(cols_ref.at[pair], slot * step + frame * 3 * channels, channels, half, values)
        for i, (out_hbm, out_ref, w_ref, cols_ref) in enumerate(
            ((one_hbm, one_ref, w_one_ref, one_cols_ref), (two_hbm, two_ref, w_two_ref, two_cols_ref))
        ):
            for row in range(out_ref.shape[1]):
                out_ref[pair, row] = jnp.dot(
                    w_ref[...], cols_ref[pair, row * step : (row + 3) * step, :], preferred_element_type=F32
                )
            copies.append(pltpu.make_async_copy(out_ref.at[pair], out_hbm.at[pair], sems.at[pair, i]))
            copies[-1].start()
    for copy in copies:
        copy.wait()


def past_sums(place, session_of, counts, own, above, below, w_one, w_two):
    _, rows, sessions, frames, channels, width = own.shape
    pairs, lanes, step = sessions // 2, 2 * width, frames * 3 * channels
    vmem, smem = pl.BlockSpec(memory_space=pltpu.VMEM), pl.BlockSpec(memory_space=pltpu.SMEM)
    return pl.pallas_call(
        past_kernel,
        in_specs=[smem, smem, smem, vmem, vmem, vmem, vmem, vmem],
        out_specs=[pl.BlockSpec(memory_space=pltpu.HBM)] * 2,
        out_shape=[
            pltpu.HBM((pairs, rows + 2, channels, lanes), F32),
            pltpu.HBM((pairs, rows, channels, lanes), F32),
        ],
        scratch_shapes=[
            pltpu.VMEM((pairs, (rows + 4) * step, lanes), BF16),
            pltpu.VMEM((pairs, (rows + 2) * step, lanes), BF16),
            pltpu.VMEM((pairs, rows + 2, channels, lanes), F32),
            pltpu.VMEM((pairs, rows, channels, lanes), F32),
            pltpu.SemaphoreType.DMA((pairs, 2)),
        ],
        compiler_params=pltpu.CompilerParams(vmem_limit_bytes=24 * 1024 * 1024),
        cost_estimate=pl.CostEstimate(flops=4 * 10**9, bytes_accessed=6 * 10**6, transcendentals=0),
        name="past_sums",
    )(place, session_of, counts, own, below, above, w_one, w_two)


def frame_row(ref, row, session, parts):
    return jnp.concatenate([ref[row * parts + q, session].astype(F32) for q in range(parts)], axis=0)


def store_act(cols_ref, pair, slot, act):
    channels, width = act.shape[0], act.shape[1] // 2
    for half in range(2):
        store_taps(cols_ref.at[pair], slot * 3 * channels, channels, half, act[:, half * width : (half + 1) * width])


def own_kernel(own_ref, one_hbm, two_hbm, w_one_hbm, w_two_hbm, g_one_ref, g_two_ref, cols_ref, acts_ref, one_ref, two_ref, w_one_ref, w_two_ref, sems):
    channels = w_one_hbm.shape[0]
    parts = channels // own_ref.shape[2]
    rows = own_ref.shape[0] // parts
    step = 3 * channels
    copies = [
        pltpu.make_async_copy(source, target, sems.at[i])
        for i, (source, target) in enumerate(
            ((w_one_hbm, w_one_ref), (one_hbm, one_ref), (two_hbm, two_ref), (w_two_hbm, w_two_ref))
        )
    ]
    for copy in copies:
        copy.start()
    g_one, g_two = g_one_ref[...], g_two_ref[...]
    pairs = own_ref.shape[1] // 2
    for pair in range(pairs):
        for row in range(rows):
            for half in range(2):
                act = norm_silu(frame_row(own_ref, row, 2 * pair + half, parts), g_one)
                store_taps(cols_ref.at[pair], row * step, channels, half, act)
    copies[0].wait()
    copies[1].wait()
    for pair in range(pairs):
        for row in range(rows - 2):
            hidden = one_ref[pair, row + 2] + jnp.dot(
                w_one_ref[...], cols_ref[pair, row * step : (row + 3) * step, :], preferred_element_type=F32
            )
            store_act(acts_ref, pair, row, norm_silu(hidden, g_two))
    copies[2].wait()
    copies[3].wait()


def own_rows(own, one, two, w_one, w_two, g_one, g_two):
    pairs, rows, channels, lanes = two.shape
    step = 3 * channels
    vmem, hbm = pl.BlockSpec(memory_space=pltpu.VMEM), pl.BlockSpec(memory_space=pltpu.HBM)
    one, two, w_one, w_two = (pltpu.with_memory_space_constraint(x, pltpu.HBM) for x in (one, two, w_one, w_two))
    return pl.pallas_call(
        own_kernel,
        in_specs=[vmem] + [hbm] * 4 + [vmem] * 2,
        out_specs=[vmem] * 6,
        out_shape=[
            jax.ShapeDtypeStruct((pairs, rows * step, lanes), BF16),
            jax.ShapeDtypeStruct((pairs, (rows - 2) * step, lanes), BF16),
            jax.ShapeDtypeStruct(one.shape, F32),
            jax.ShapeDtypeStruct(two.shape, F32),
            jax.ShapeDtypeStruct(w_one.shape, BF16),
            jax.ShapeDtypeStruct(w_two.shape, BF16),
        ],
        scratch_shapes=[pltpu.SemaphoreType.DMA((4,))],
        compiler_params=pltpu.CompilerParams(vmem_limit_bytes=16 * 1024 * 1024),
        cost_estimate=pl.CostEstimate(flops=10**9, bytes_accessed=4 * 10**6, transcendentals=10**6),
        name="own_rows",
    )(own, one, two, w_one, w_two, g_one, g_two)


def side_kernel(place_ref, session_of_ref, active_ref, halo_ref, own_ref, own_cols_ref, mid_acts_ref, one_ref, two_ref, w_one_ref, w_two_ref, g_one_ref, g_two_ref, *rest, top, bands):
    out_ref, cols_ref, edge_ref = rest[-3:]
    channels = w_one_ref.shape[0]
    sessions, part = own_ref.shape[1], own_ref.shape[2]
    width = own_ref.shape[3]
    parts = channels // part
    rows = own_ref.shape[0] // parts
    step = 3 * channels
    inside = ((place_ref[1] > 0) if top else (place_ref[1] < bands - 1)).astype(F32)
    g_one, g_two = g_one_ref[...], g_two_ref[...]


    def split_dot(w_ref, row, side, inner):
        count = 2 - row if top else 1 + row
        if top:
            near = side[(2 - count) * step : 2 * step, :]
            far = inner[: (3 - count) * step, :]
            near_w, far_w = w_ref[:, : count * step], w_ref[:, count * step :]
        else:
            near = side[: count * step, :]
            far = inner[(count - 1) * step : 2 * step, :]
            near_w, far_w = w_ref[:, (3 - count) * step :], w_ref[:, : (3 - count) * step]
        return jnp.dot(near_w, near, preferred_element_type=F32) + jnp.dot(far_w, far, preferred_element_type=F32)

    for pair in range(sessions // 2):
        for row in range(2):
            for half in range(2):
                act = norm_silu(frame_row(halo_ref, row, 2 * pair + half, parts), g_one)
                store_taps(cols_ref.at[pair], row * step, channels, half, act)
    first = 0 if top else rows
    from_row = 0 if top else rows - 2
    for pair in range(sessions // 2):
        for row in range(2):
            hidden = one_ref[pair, first + row] + split_dot(w_one_ref, row, cols_ref.at[pair], own_cols_ref.at[pair, pl.ds(from_row * step, 2 * step)])
            act = norm_silu(hidden, g_two)
            if row == (0 if top else 1):
                act = act * inside
            store_act(edge_ref, pair, row, act)
    first = 0 if top else rows - 2
    for pair in range(sessions // 2):
        for row in range(2):
            hidden = two_ref[pair, first + row] + split_dot(w_two_ref, row, edge_ref.at[pair], mid_acts_ref.at[pair])
            for half in range(2):
                session = 2 * pair + half
                active = active_ref[session_of_ref[place_ref[0] * sessions + session]].astype(F32)
                total = active * (
                    frame_row(own_ref, first + row, session, parts) + hidden[:, half * width : (half + 1) * width]
                )
                for q in range(parts):
                    out_ref[(first + row) * parts + q, session] = total[q * part : (q + 1) * part].astype(BF16)


def side_rows(top, bands, place, session_of, active, halo, own, held, g_one, g_two, earlier=None):
    own_cols, mid_acts, one, two, w_one, w_two = held
    pairs, rows, channels, lanes = two.shape
    step = 3 * channels
    vmem, smem = pl.BlockSpec(memory_space=pltpu.VMEM), pl.BlockSpec(memory_space=pltpu.SMEM)
    operands = [place, session_of, active, halo, own, own_cols, mid_acts, one, two, w_one, w_two, g_one, g_two]
    operands += [] if earlier is None else [earlier]
    return pl.pallas_call(
        functools.partial(side_kernel, top=top, bands=bands),
        in_specs=[smem] * 3 + [vmem] * (len(operands) - 3),
        out_specs=vmem,
        out_shape=jax.ShapeDtypeStruct(own.shape, BF16),
        input_output_aliases={} if earlier is None else {len(operands) - 1: 0},
        scratch_shapes=[pltpu.VMEM((pairs, 2 * step, lanes), BF16), pltpu.VMEM((pairs, 2 * step, lanes), BF16)],
        compiler_params=pltpu.CompilerParams(vmem_limit_bytes=16 * 1024 * 1024),
        cost_estimate=pl.CostEstimate(flops=10**9, bytes_accessed=4 * 10**6, transcendentals=10**6),
        name="top_rows" if top else "bottom_rows",
    )(*operands)


def weights_kernel(one_ref, two_ref, past_one_ref, past_two_ref, new_one_ref, new_two_ref):
    third = one_ref.shape[1] // 3
    new = third // 3
    past = third - new
    for source, past_out, new_out in ((one_ref, past_one_ref, new_one_ref), (two_ref, past_two_ref, new_two_ref)):
        values = source[...]
        rows = [values[:, dy * third : (dy + 1) * third] for dy in range(3)]
        past_out[...] = jnp.concatenate([row[:, :past] for row in rows], axis=1)
        new_out[...] = jnp.concatenate([row[:, past:] for row in rows], axis=1)


def split_weights(one, two):
    channels, columns = one.shape
    past = jax.ShapeDtypeStruct((channels, columns // 3 * 2), one.dtype)
    new = jax.ShapeDtypeStruct((channels, columns // 3), one.dtype)
    return pl.pallas_call(
        weights_kernel,
        out_shape=[past, past, new, new],
        compiler_params=pltpu.CompilerParams(vmem_limit_bytes=16 * 1024 * 1024),
        cost_estimate=pl.CostEstimate(flops=0, bytes_accessed=2 * 10**6, transcendentals=0),
        name="split_weights",
    )(one, two)


def send_kernel(slots_ref, in_ref, out_hbm, buf_ref, sems):
    chunk = in_ref.shape[0] // sems.shape[0]
    copies = []
    for i in range(sems.shape[0]):
        for slot in range(i * chunk, (i + 1) * chunk):
            buf_ref[slot] = in_ref[slots_ref[slot]]
        block = pl.ds(i * chunk, chunk)
        copies.append(pltpu.make_async_copy(buf_ref.at[block], out_hbm.at[block], sems.at[i]))
        copies[-1].start()
    for copy in copies:
        copy.wait()


def take_to_hbm(pieces, slots):
    return pl.pallas_call(
        send_kernel,
        in_specs=[pl.BlockSpec(memory_space=pltpu.SMEM), pl.BlockSpec(memory_space=pltpu.VMEM)],
        out_specs=pl.BlockSpec(memory_space=pltpu.HBM),
        out_shape=pltpu.HBM(pieces.shape, pieces.dtype),
        scratch_shapes=[pltpu.VMEM(pieces.shape, pieces.dtype), pltpu.SemaphoreType.DMA((4,))],
        compiler_params=pltpu.CompilerParams(vmem_limit_bytes=4 * 1024 * 1024),
        name="take_to_hbm",
    )(slots, pieces)


def take_kernel(slots_ref, in_ref, out_ref):
    for slot in range(in_ref.shape[0]):
        out_ref[slot] = in_ref[slots_ref[slot]]


def take_in_vmem(pieces, slots):
    vmem = pl.BlockSpec(memory_space=pltpu.VMEM)
    return pl.pallas_call(
        take_kernel,
        in_specs=[pl.BlockSpec(memory_space=pltpu.SMEM), vmem],
        out_specs=vmem,
        out_shape=jax.ShapeDtypeStruct(pieces.shape, pieces.dtype),
        compiler_params=pltpu.CompilerParams(vmem_limit_bytes=4 * 1024 * 1024),
        name="take_in_vmem",
    )(slots, pieces)


def exchange(pieces):
    return lax.all_to_all(pieces, "sess", 0, 0, tiled=True)


def local(frame, cache, holder_map, counts, active, weight_one, weight_two, gain_one, gain_two):
    sess_count, band_count = lax.axis_size("sess"), lax.axis_size("band")
    me, band = lax.axis_index("sess"), lax.axis_index("band")
    sessions, channels, rows, width = frame.shape
    parts = sess_count // rows
    part = channels // parts
    down = [(i, i + 1) for i in range(band_count - 1)]
    up = [(i + 1, i) for i in range(band_count - 1)]

    ids = jnp.arange(sess_count * sessions, dtype=jnp.int32)
    session_of = jnp.sum(jnp.where(holder_map[None, :] == ids[:, None], ids[None, :], 0), axis=1)
    place = jnp.stack([me, band]).astype(jnp.int32)

    cut = frame.reshape(sessions, parts, part, rows, width).transpose(3, 1, 0, 2, 4)
    cut, cache = lax.optimization_barrier((cut, cache))
    spread = exchange(cut.reshape(sess_count, sessions, part, width))

    own = cache.transpose(1, 4, 0, 2, 3, 5)
    below = lax.ppermute(jnp.concatenate([own[0, :2], own[1, :1]]), "band", up)
    above = lax.ppermute(jnp.concatenate([own[0, rows - 2 :], own[1, rows - 1 :]]), "band", down)
    past_one, past_two, new_one, new_two = split_weights(weight_one, weight_two)
    one, two = past_sums(place, session_of, counts, own, above, below, past_one, past_two)

    sorted_pieces = take_to_hbm(spread.reshape(-1, part, width), session_of)
    held = exchange(sorted_pieces.reshape(sess_count, sessions, part, width))
    held, one, two = lax.optimization_barrier((held, one, two))
    half = sess_count - 2 * parts
    held_above = lax.ppermute(held[half:], "band", down)
    held_below = lax.ppermute(held[: 2 * parts], "band", up)
    gains = gain_one[:, None], gain_two[:, None]
    inner = own_rows(held, one, two, new_one, new_two, *gains)
    upper = side_rows(True, band_count, place, session_of, active, held_above, held, inner, *gains)
    result = side_rows(False, band_count, place, session_of, active, held_below, held, inner, *gains, earlier=upper)

    spread_result = exchange(result)
    home_pieces = take_in_vmem(spread_result.reshape(-1, part, width), holder_map)
    home = exchange(home_pieces.reshape(sess_count, sessions, part, width))
    home = home.reshape(rows, parts, sessions, part, width).transpose(2, 1, 3, 0, 4)
    return home.reshape(sessions, channels, rows, width)


def solution(mesh):
    return jax.shard_map(
        local,
        mesh=mesh,
        in_specs=(
            P("sess", None, "band", None),
            P("sess", None, None, None, "band", None),
            P(),
            P(),
            P(),
            P(),
            P(),
            P(),
            P(),
        ),
        out_specs=P("sess", None, "band", None),
        check_vma=False,
    )
```

```python
import functools

import jax
import jax.numpy as jnp
from jax import lax
from jax.experimental import pallas as pl
from jax.experimental.pallas import tpu as pltpu
from jax.sharding import PartitionSpec as P

F32 = jnp.float32
BF16 = jnp.bfloat16


def three_taps(values):
    width = values.shape[1]
    column = lax.broadcasted_iota(jnp.int32, values.shape, 1)
    before = jnp.where(column == 0, 0.0, pltpu.roll(values, 1, 1))
    after = jnp.where(column == width - 1, 0.0, pltpu.roll(values, width - 1, 1))
    return before.astype(BF16), values.astype(BF16), after.astype(BF16)


def store_taps(cols_ref, at, channels, half, values):
    width = values.shape[1]
    for tap, moved in enumerate(three_taps(values)):
        cols_ref[at + tap * channels : at + (tap + 1) * channels, half * width : (half + 1) * width] = moved


def norm_silu(values, gain):
    mean_square = jnp.mean(values * values, axis=0, keepdims=True)
    scaled = values * lax.rsqrt(mean_square + 1e-06) * gain
    half = 0.5 * scaled
    return half + half * jnp.tanh(half)


def past_kernel(place_ref, session_of_ref, counts_ref, own_ref, below_ref, above_ref, w_one_ref, w_two_ref, one_hbm, two_hbm, one_cols_ref, two_cols_ref, one_ref, two_ref, sems):
    _, rows, sessions, frames, channels, _ = own_ref.shape
    step = frames * 3 * channels
    copies = []
    for pair in range(sessions // 2):
        for half in range(2):
            session = 2 * pair + half
            count = counts_ref[session_of_ref[place_ref[0] * sessions + session]]
            for frame in range(frames):
                live = (frame >= 2 - count).astype(F32)
                one_rows = [above_ref.at[0], above_ref.at[1]] + [own_ref.at[0, r] for r in range(rows)] + [below_ref.at[0], below_ref.at[1]]
                two_rows = [above_ref.at[2]] + [own_ref.at[1, r] for r in range(rows)] + [below_ref.at[2]]
                for cols_ref, row_refs in ((one_cols_ref, one_rows), (two_cols_ref, two_rows)):
                    for slot, row_ref in enumerate(row_refs):
                        values = row_ref[session, frame].astype(F32) * live
                        store_taps(cols_ref.at[pair], slot * step + frame * 3 * channels, channels, half, values)
        for i, (out_hbm, out_ref, w_ref, cols_ref) in enumerate(
            ((one_hbm, one_ref, w_one_ref, one_cols_ref), (two_hbm, two_ref, w_two_ref, two_cols_ref))
        ):
            for row in range(out_ref.shape[1]):
                out_ref[pair, row] = jnp.dot(
                    w_ref[...], cols_ref[pair, row * step : (row + 3) * step, :], preferred_element_type=F32
                )
            copies.append(pltpu.make_async_copy(out_ref.at[pair], out_hbm.at[pair], sems.at[pair, i]))
            copies[-1].start()
    for copy in copies:
        copy.wait()


def past_sums(place, session_of, counts, own, above, below, w_one, w_two):
    _, rows, sessions, frames, channels, width = own.shape
    pairs, lanes, step = sessions // 2, 2 * width, frames * 3 * channels
    vmem, smem = pl.BlockSpec(memory_space=pltpu.VMEM), pl.BlockSpec(memory_space=pltpu.SMEM)
    return pl.pallas_call(
        past_kernel,
        in_specs=[smem, smem, smem, vmem, vmem, vmem, vmem, vmem],
        out_specs=[pl.BlockSpec(memory_space=pltpu.HBM)] * 2,
        out_shape=[
            pltpu.HBM((pairs, rows + 2, channels, lanes), F32),
            pltpu.HBM((pairs, rows, channels, lanes), F32),
        ],
        scratch_shapes=[
            pltpu.VMEM((pairs, (rows + 4) * step, lanes), BF16),
            pltpu.VMEM((pairs, (rows + 2) * step, lanes), BF16),
            pltpu.VMEM((pairs, rows + 2, channels, lanes), F32),
            pltpu.VMEM((pairs, rows, channels, lanes), F32),
            pltpu.SemaphoreType.DMA((pairs, 2)),
        ],
        compiler_params=pltpu.CompilerParams(vmem_limit_bytes=24 * 1024 * 1024),
        cost_estimate=pl.CostEstimate(flops=4 * 10**9, bytes_accessed=6 * 10**6, transcendentals=0),
        name="past_sums",
    )(place, session_of, counts, own, below, above, w_one, w_two)


def frame_row(ref, row, session, parts):
    return jnp.concatenate([ref[row * parts + q, session].astype(F32) for q in range(parts)], axis=0)


def store_act(cols_ref, pair, slot, act):
    channels, width = act.shape[0], act.shape[1] // 2
    for half in range(2):
        store_taps(cols_ref.at[pair], slot * 3 * channels, channels, half, act[:, half * width : (half + 1) * width])


def own_kernel(own_ref, one_hbm, two_hbm, w_one_hbm, w_two_hbm, g_one_ref, g_two_ref, cols_ref, acts_ref, one_ref, two_ref, w_one_ref, w_two_ref, sems):
    channels = w_one_hbm.shape[0]
    parts = channels // own_ref.shape[2]
    rows = own_ref.shape[0] // parts
    step = 3 * channels
    copies = [
        pltpu.make_async_copy(source, target, sems.at[i])
        for i, (source, target) in enumerate(
            ((w_one_hbm, w_one_ref), (one_hbm, one_ref), (two_hbm, two_ref), (w_two_hbm, w_two_ref))
        )
    ]
    for copy in copies:
        copy.start()
    g_one, g_two = g_one_ref[...], g_two_ref[...]
    pairs = own_ref.shape[1] // 2
    for pair in range(pairs):
        for row in range(rows):
            for half in range(2):
                act = norm_silu(frame_row(own_ref, row, 2 * pair + half, parts), g_one[:, : own_ref.shape[3]])
                store_taps(cols_ref.at[pair], row * step, channels, half, act)
    copies[0].wait()
    copies[1].wait()
    for pair in range(pairs):
        for row in range(rows - 2):
            hidden = one_ref[pair, row + 2] + jnp.dot(
                w_one_ref[...], cols_ref[pair, row * step : (row + 3) * step, :], preferred_element_type=F32
            )
            store_act(acts_ref, pair, row, norm_silu(hidden, g_two))
    copies[2].wait()
    copies[3].wait()


def own_rows(own, one, two, w_one, w_two, g_one, g_two):
    pairs, rows, channels, lanes = two.shape
    step = 3 * channels
    vmem, hbm = pl.BlockSpec(memory_space=pltpu.VMEM), pl.BlockSpec(memory_space=pltpu.HBM)
    one, two, w_one, w_two = (pltpu.with_memory_space_constraint(x, pltpu.HBM) for x in (one, two, w_one, w_two))
    return pl.pallas_call(
        own_kernel,
        in_specs=[vmem] + [hbm] * 4 + [vmem] * 2,
        out_specs=[vmem] * 6,
        out_shape=[
            jax.ShapeDtypeStruct((pairs, rows * step, lanes), BF16),
            jax.ShapeDtypeStruct((pairs, (rows - 2) * step, lanes), BF16),
            jax.ShapeDtypeStruct(one.shape, F32),
            jax.ShapeDtypeStruct(two.shape, F32),
            jax.ShapeDtypeStruct(w_one.shape, BF16),
            jax.ShapeDtypeStruct(w_two.shape, BF16),
        ],
        scratch_shapes=[pltpu.SemaphoreType.DMA((4,))],
        compiler_params=pltpu.CompilerParams(vmem_limit_bytes=16 * 1024 * 1024),
        cost_estimate=pl.CostEstimate(flops=10**9, bytes_accessed=4 * 10**6, transcendentals=10**6),
        name="own_rows",
    )(own, one, two, w_one, w_two, g_one, g_two)


def side_kernel(place_ref, session_of_ref, active_ref, halo_ref, own_ref, own_cols_ref, mid_acts_ref, one_ref, two_ref, w_one_ref, w_two_ref, g_one_ref, g_two_ref, *rest, top, bands):
    out_ref, cols_ref, edge_ref = rest[-3:]
    channels = w_one_ref.shape[0]
    sessions, part = own_ref.shape[1], own_ref.shape[2]
    width = own_ref.shape[3]
    parts = channels // part
    rows = own_ref.shape[0] // parts
    step = 3 * channels
    inside = ((place_ref[1] > 0) if top else (place_ref[1] < bands - 1)).astype(F32)
    g_one, g_two = g_one_ref[...], g_two_ref[...]


    def split_dot(w_ref, row, side, inner):
        count = 2 - row if top else 1 + row
        if top:
            near = side[(2 - count) * step : 2 * step, :]
            far = inner[: (3 - count) * step, :]
            near_w, far_w = w_ref[:, : count * step], w_ref[:, count * step :]
        else:
            near = side[: count * step, :]
            far = inner[(count - 1) * step : 2 * step, :]
            near_w, far_w = w_ref[:, (3 - count) * step :], w_ref[:, : (3 - count) * step]
        return jnp.dot(near_w, near, preferred_element_type=F32) + jnp.dot(far_w, far, preferred_element_type=F32)

    for pair in range(sessions // 2):
        for row in range(2):
            for half in range(2):
                act = norm_silu(frame_row(halo_ref, row, 2 * pair + half, parts), g_one[:, :width])
                store_taps(cols_ref.at[pair], row * step, channels, half, act)
    first = 0 if top else rows
    from_row = 0 if top else rows - 2
    for pair in range(sessions // 2):
        for row in range(2):
            hidden = one_ref[pair, first + row] + split_dot(w_one_ref, row, cols_ref.at[pair], own_cols_ref.at[pair, pl.ds(from_row * step, 2 * step)])
            act = norm_silu(hidden, g_two)
            if row == (0 if top else 1):
                act = act * inside
            store_act(edge_ref, pair, row, act)
    first = 0 if top else rows - 2
    for pair in range(sessions // 2):
        for row in range(2):
            hidden = two_ref[pair, first + row] + split_dot(w_two_ref, row, edge_ref.at[pair], mid_acts_ref.at[pair])
            for half in range(2):
                session = 2 * pair + half
                active = active_ref[session_of_ref[place_ref[0] * sessions + session]].astype(F32)
                total = active * (
                    frame_row(own_ref, first + row, session, parts) + hidden[:, half * width : (half + 1) * width]
                )
                for q in range(parts):
                    out_ref[(first + row) * parts + q, session] = total[q * part : (q + 1) * part].astype(BF16)


def side_rows(top, bands, place, session_of, active, halo, own, held, g_one, g_two, earlier=None):
    own_cols, mid_acts, one, two, w_one, w_two = held
    pairs, rows, channels, lanes = two.shape
    step = 3 * channels
    vmem, smem = pl.BlockSpec(memory_space=pltpu.VMEM), pl.BlockSpec(memory_space=pltpu.SMEM)
    operands = [place, session_of, active, halo, own, own_cols, mid_acts, one, two, w_one, w_two, g_one, g_two]
    operands += [] if earlier is None else [earlier]
    return pl.pallas_call(
        functools.partial(side_kernel, top=top, bands=bands),
        in_specs=[smem] * 3 + [vmem] * (len(operands) - 3),
        out_specs=vmem,
        out_shape=jax.ShapeDtypeStruct(own.shape, BF16),
        input_output_aliases={} if earlier is None else {len(operands) - 1: 0},
        scratch_shapes=[pltpu.VMEM((pairs, 2 * step, lanes), BF16), pltpu.VMEM((pairs, 2 * step, lanes), BF16)],
        compiler_params=pltpu.CompilerParams(vmem_limit_bytes=16 * 1024 * 1024),
        cost_estimate=pl.CostEstimate(flops=10**9, bytes_accessed=4 * 10**6, transcendentals=10**6),
        name="top_rows" if top else "bottom_rows",
    )(*operands)


def weights_kernel(one_ref, two_ref, past_one_ref, past_two_ref, new_one_ref, new_two_ref):
    third = one_ref.shape[1] // 3
    new = third // 3
    past = third - new
    for source, past_out, new_out in ((one_ref, past_one_ref, new_one_ref), (two_ref, past_two_ref, new_two_ref)):
        values = source[...]
        rows = [values[:, dy * third : (dy + 1) * third] for dy in range(3)]
        past_out[...] = jnp.concatenate([row[:, :past] for row in rows], axis=1)
        new_out[...] = jnp.concatenate([row[:, past:] for row in rows], axis=1)


def split_weights(one, two):
    channels, columns = one.shape
    past = jax.ShapeDtypeStruct((channels, columns // 3 * 2), one.dtype)
    new = jax.ShapeDtypeStruct((channels, columns // 3), one.dtype)
    return pl.pallas_call(
        weights_kernel,
        out_shape=[past, past, new, new],
        compiler_params=pltpu.CompilerParams(vmem_limit_bytes=16 * 1024 * 1024),
        cost_estimate=pl.CostEstimate(flops=0, bytes_accessed=2 * 10**6, transcendentals=0),
        name="split_weights",
    )(one, two)


def take_slots(pieces, slots):
    return lax.gather(
        pieces,
        slots[:, None],
        lax.GatherDimensionNumbers(offset_dims=(1, 2), collapsed_slice_dims=(0,), start_index_map=(0,)),
        slice_sizes=(1,) + pieces.shape[1:],
        unique_indices=True,
        mode=lax.GatherScatterMode.CLIP,
    )


def take_kernel(slots_ref, in_ref, out_ref):
    for slot in range(in_ref.shape[0]):
        out_ref[slot] = in_ref[slots_ref[slot]]


def take_in_vmem(pieces, slots):
    vmem = pl.BlockSpec(memory_space=pltpu.VMEM)
    return pl.pallas_call(
        take_kernel,
        in_specs=[pl.BlockSpec(memory_space=pltpu.SMEM), vmem],
        out_specs=vmem,
        out_shape=jax.ShapeDtypeStruct(pieces.shape, pieces.dtype),
        compiler_params=pltpu.CompilerParams(vmem_limit_bytes=4 * 1024 * 1024),
        name="take_in_vmem",
    )(slots, pieces)


def exchange(pieces):
    return lax.all_to_all(pieces, "sess", 0, 0, tiled=True)


def local(frame, cache, holder_map, counts, active, weight_one, weight_two, gain_one, gain_two):
    sess_count, band_count = lax.axis_size("sess"), lax.axis_size("band")
    me, band = lax.axis_index("sess"), lax.axis_index("band")
    sessions, channels, rows, width = frame.shape
    parts = sess_count // rows
    part = channels // parts
    down = [(i, i + 1) for i in range(band_count - 1)]
    up = [(i + 1, i) for i in range(band_count - 1)]

    ids = jnp.arange(sess_count * sessions, dtype=jnp.int32)
    session_of = jnp.sum(jnp.where(holder_map[None, :] == ids[:, None], ids[None, :], 0), axis=1)
    place = jnp.stack([me, band]).astype(jnp.int32)

    cut = frame.reshape(sessions, parts, part, rows, width).transpose(3, 1, 0, 2, 4)
    cut, cache = lax.optimization_barrier((cut, cache))
    spread = exchange(cut.reshape(sess_count, sessions, part, width))

    own = cache.transpose(1, 4, 0, 2, 3, 5)
    below = lax.ppermute(jnp.concatenate([own[0, :2], own[1, :1]]), "band", up)
    above = lax.ppermute(jnp.concatenate([own[0, rows - 2 :], own[1, rows - 1 :]]), "band", down)
    past_one, past_two, new_one, new_two = split_weights(weight_one, weight_two)
    one, two = past_sums(place, session_of, counts, own, above, below, past_one, past_two)

    sorted_pieces = take_slots(spread.reshape(-1, part, width), session_of)
    held = exchange(sorted_pieces.reshape(sess_count, sessions, part, width))
    held, one, two = lax.optimization_barrier((held, one, two))
    half = sess_count - 2 * parts
    held_above = lax.ppermute(held[half:], "band", down)
    held_below = lax.ppermute(held[: 2 * parts], "band", up)
    gains = [jnp.broadcast_to(gain[:, None], (channels, 2 * width)) for gain in (gain_one, gain_two)]
    inner = own_rows(held, one, two, new_one, new_two, *gains)
    upper = side_rows(True, band_count, place, session_of, active, held_above, held, inner, *gains)
    result = side_rows(False, band_count, place, session_of, active, held_below, held, inner, *gains, earlier=upper)

    spread_result = exchange(result)
    home_pieces = take_in_vmem(spread_result.reshape(-1, part, width), holder_map)
    home = exchange(home_pieces.reshape(sess_count, sessions, part, width))
    home = home.reshape(rows, parts, sessions, part, width).transpose(2, 1, 3, 0, 4)
    return home.reshape(sessions, channels, rows, width)


def solution(mesh):
    return jax.shard_map(
        local,
        mesh=mesh,
        in_specs=(
            P("sess", None, "band", None),
            P("sess", None, None, None, "band", None),
            P(),
            P(),
            P(),
            P(),
            P(),
            P(),
            P(),
        ),
        out_specs=P("sess", None, "band", None),
        check_vma=False,
    )
```
